32 devices in a mesh: groups: 2 (over x), pencil: 16 (over z, y, core).
Axes of the slice: x: 2, y: 2, z: 4, core: 2. Of those that a mesh axis runs over, the one named last changes fastest.
Arguments:
- krylov_vector: bfloat16 [10, 512, 256, 128], P('groups', 'pencil'), parts along dimension 0, may hold values from -6 to 6
- base_wave: bfloat16 [10, 256, 512], P('groups', 'pencil'), parts along dimension 0, may hold values from -3 to 3
- radial_inverse: bfloat16 [258, 64, 64], P('groups'), parts along dimension 0, may hold values from -0.5 to 1.15
- step_counts: int32 [10], P('groups'), parts along dimension 0, may hold values from 1 to 3, as said below
- azimuth_shift: int32 [2], P('groups'), parts along dimension 0, may hold values from 0 to 255
- phase_tangent: bfloat16 [1024, 256, 128], P(('groups', 'pencil')), parts along dimension 0, may hold values from -1 to 1
Outputs:
- shooting: float32 [10, 512, 256, 128], P('groups', 'pencil'), parts along dimension 0
- phase_value: float32 [2], P('groups'), parts along dimension 0
The draws below stay inside these ranges and needn't reach their ends.
There are 2 independent parts, one for each index of `groups`. The reference program is written for one: setup_inputs(seed, part) draws one part's arguments, and reference() takes and returns one part's arrays. A program takes and returns all parts, laid end to end along the dimension named above; each array names one. Nothing has to cross between parts.
Inputs may be any that keep to these rules, and one draw needn't show every extreme that they name: `step_counts`: some segment takes exactly 3 steps.
All inputs are finite; a program needn't handle non-finite values.
Results may differ from the reference program's by a relative error of at most 0.006.
Values may be sent and summed in bfloat16 or wider, within the bound.
A program may use at most 192 MiB of HBM per device.

```python
import math
import jax
import jax.numpy as jnp
from jax import lax

R = 64
M = 256
Z = 512
K = 2
S = 5
NSTEP = 3
KR = 128


def draw_radial_inverse(key, part):
    key = jax.random.fold_in(key, 11)
    key_diagonal, key_off = jax.random.split(key)
    waves = M // 2 + 1
    diagonal = jax.random.uniform(key_diagonal, (waves, R), jnp.float32, 0.85, 1.15)
    off_part = jax.random.uniform(key_off, (waves, R, R), jnp.float32, -1.0, 1.0) * (0.5 / math.sqrt(R))
    identity = jnp.eye(R, dtype=jnp.float32)
    return (off_part * (1.0 - identity) + diagonal[:, :, None] * identity).astype(jnp.bfloat16)


def draw_step_counts(key, part):
    key = jax.random.fold_in(key, 23)
    key_counts, key_chosen = jax.random.split(key)
    counts = jax.random.randint(key_counts, (S,), 1, NSTEP + 1)
    chosen = jax.random.randint(key_chosen, (), 0, S)
    return jnp.where(jnp.arange(S) == chosen, NSTEP, counts).astype(jnp.int32)


def draw_phase_tangent(key, part):
    key = jax.random.fold_in(key, 37)
    key_entries, key_rough = jax.random.split(key)
    rising = (3.0 ** (jnp.arange(Z, dtype=jnp.float32) / (Z - 1)))[:, None, None]
    roughness = jax.random.uniform(key_rough, (Z, M, K * R), jnp.float32, 0.5, 2.0)
    entries = jnp.clip(jax.random.normal(key_entries, (Z, M, K * R), jnp.float32), -4.0, 4.0)
    return (entries * roughness * rising * (0.6 / math.sqrt(Z * M * K * R))).astype(jnp.bfloat16)


def shard_levels(rng, dims, pieces, smallest, high):
    def one(position, shards_of):
        heights = jax.random.uniform(jax.random.fold_in(jax.random.fold_in(rng, 6), position), (shards_of,), jnp.float32, smallest / len(pieces), high / len(pieces))
        return jnp.repeat(jnp.exp(heights), dims[position] // shards_of).reshape((-1,) + (1,) * (len(dims) - position - 1))

    level = one(*pieces[0])
    for cut in pieces[1:]:
        level = level * one(*cut)
    return level


def normal_values(own_key, dims, spread, reach, cuts=(), held_as=jnp.bfloat16):
    gain = shard_levels(own_key, dims, cuts, -0.22, 0.18) if cuts else 1.0
    drawn = jax.random.normal(own_key, dims, jnp.float32) * spread * gain
    return jnp.minimum(jnp.maximum(drawn, -reach), reach).astype(held_as)


def setup_inputs(seed: int = 0, part: int = 0) -> dict:
    key_of = jax.random.split(jax.random.key(seed), 7)
    part_keys = jax.random.split(jax.random.fold_in(key_of[6], part), 7)
    return {
        "krylov_vector": normal_values(part_keys[0], (S, Z, M, KR), 1.0, 6.0, ((1, 16),)),
        "base_wave": normal_values(part_keys[1], (S, M, Z), 0.5, 3.0, ((1, 16),)),
        "radial_inverse": draw_radial_inverse(jax.random.fold_in(jax.random.fold_in(key_of[6], part), 71), part),
        "step_counts": draw_step_counts(jax.random.fold_in(jax.random.fold_in(key_of[6], part), 71), part),
        "azimuth_shift": jax.random.randint(part_keys[4], (1,), 0, M).astype(jnp.int32),
        "phase_tangent": draw_phase_tangent(jax.random.fold_in(jax.random.fold_in(key_of[6], part), 71), part),
    }


viscosity = 2e-06
step_size = 0.4

def fourier_table(length):
    points = jnp.arange(length, dtype=jnp.int32)
    columns = jnp.arange(length, dtype=jnp.int32)
    wave_numbers = (columns + 1) // 2
    phase_index = points[:, None] * wave_numbers[None, :] % length
    angles = phase_index.astype(jnp.float32) * (2.0 * jnp.pi / length)
    cosine_col = (columns % 2 == 1) | (columns == 0)
    edge_col = (columns == 0) | (columns == length - 1)
    scales = jnp.where(edge_col, 1.0 / jnp.sqrt(jnp.float32(length)), jnp.sqrt(jnp.float32(2.0 / length)))
    values = jnp.where(cosine_col[None, :], jnp.cos(angles), jnp.sin(angles))
    return (values * scales[None, :]).astype(jnp.float32)

def damping(axial_index, azimuth_count):
    waves_axial = (axial_index + 1) // 2
    waves_azimuth = (jnp.arange(azimuth_count, dtype=jnp.int32) + 1) // 2
    squared_sum = waves_axial[:, None] * waves_axial[:, None] + waves_azimuth[None, :] * waves_azimuth[None, :]
    return 1.0 / (1.0 + viscosity * squared_sum.astype(jnp.float32))

def expand_radial(radial_table, azimuth_count):
    half_count = azimuth_count // 2
    return jnp.concatenate([radial_table[:1], jnp.repeat(radial_table[1:half_count], 2, axis=0), radial_table[half_count:half_count + 1]], axis=0)

def advance_ref(spectral, base_plane, radial_full, table_azimuth, table_axial, damping_factor):
    physical_m = jnp.einsum('zmr,pm->zpr', spectral.astype(jnp.float32), table_azimuth).astype(jnp.bfloat16)
    physical = jnp.einsum('zpr,xz->xpr', physical_m.astype(jnp.float32), table_axial)
    product = (physical * base_plane.T.astype(jnp.float32)[:, :, None]).astype(jnp.bfloat16)
    returned = jnp.einsum('xpr,xz->zpr', product.astype(jnp.float32), table_axial).astype(jnp.bfloat16)
    tendency = jnp.einsum('zpr,pm->zmr', returned.astype(jnp.float32), table_azimuth)
    updated = (spectral.astype(jnp.float32) + step_size * tendency).astype(jnp.bfloat16)
    shaped = updated.reshape(Z, M, K, R).astype(jnp.float32)
    applied = jnp.einsum('zmkr,mor->zmko', shaped, radial_full)
    return (applied * damping_factor[:, :, None, None]).reshape(Z, M, K * R).astype(jnp.bfloat16)

def reference(krylov_vector, base_wave, radial_inverse, step_counts, azimuth_shift, phase_tangent):
    table_azimuth = fourier_table(M).astype(jnp.bfloat16).astype(jnp.float32)
    table_axial = fourier_table(Z).astype(jnp.bfloat16).astype(jnp.float32)
    damping_factor = damping(jnp.arange(Z, dtype=jnp.int32), M)
    radial_full = expand_radial(radial_inverse, M).astype(jnp.float32)
    end_states = []
    for segment in range(S):
        current_state = krylov_vector[segment]
        for step_index in range(NSTEP):
            advanced = advance_ref(current_state, base_wave[segment], radial_full, table_azimuth, table_axial, damping_factor)
            current_state = jnp.where(step_index < step_counts[segment], advanced, current_state)
        end_states.append(current_state)
    table_full = fourier_table(M)
    physical = jnp.einsum('zmr,pm->zpr', end_states[S - 1].astype(jnp.float32), table_full, precision=lax.Precision.HIGHEST)
    rolled = jnp.roll(physical, azimuth_shift[0], axis=1)
    shifted = jnp.einsum('zpr,pm->zmr', rolled, table_full, precision=lax.Precision.HIGHEST)
    rows = [end_states[segment].astype(jnp.float32) - krylov_vector[segment + 1].astype(jnp.float32) for segment in range(S - 1)]
    rows.append(shifted - krylov_vector[0].astype(jnp.float32))
    shooting = jnp.stack(rows, axis=0)
    phase_value = jnp.sum(phase_tangent.astype(jnp.float32) * krylov_vector[0].astype(jnp.float32)).reshape(1)
    return (shooting, phase_value)
```

```python
import functools
import jax
import jax.numpy as jnp
from jax import lax
from jax.experimental import pallas as pl
from jax.experimental.pallas import tpu as pltpu
from jax.sharding import PartitionSpec as P

NSTEP = 3


viscosity = 2e-06
step_size = 0.4


def fourier_table(length):
    points = jnp.arange(length, dtype=jnp.int32)
    columns = jnp.arange(length, dtype=jnp.int32)
    wave_numbers = (columns + 1) // 2
    phase_index = points[:, None] * wave_numbers[None, :] % length
    angles = phase_index.astype(jnp.float32) * (2.0 * jnp.pi / length)
    cosine_col = (columns % 2 == 1) | (columns == 0)
    edge_col = (columns == 0) | (columns == length - 1)
    scales = jnp.where(
        edge_col, 1.0 / jnp.sqrt(jnp.float32(length)), jnp.sqrt(jnp.float32(2.0 / length))
    )
    values = jnp.where(cosine_col[None, :], jnp.cos(angles), jnp.sin(angles))
    return values * scales[None, :]


def damping(axial_index, azimuth_count):
    waves_axial = (axial_index + 1) // 2
    waves_azimuth = (jnp.arange(azimuth_count, dtype=jnp.int32) + 1) // 2
    squared_sum = (
        waves_axial[:, None] * waves_axial[:, None]
        + waves_azimuth[None, :] * waves_azimuth[None, :]
    )
    return 1.0 / (1.0 + viscosity * squared_sum.astype(jnp.float32))


def expand_radial(radial_table, azimuth_count):
    half_count = azimuth_count // 2
    return jnp.concatenate(
        [
            radial_table[:1],
            jnp.repeat(radial_table[1:half_count], 2, axis=0),
            radial_table[half_count : half_count + 1],
        ],
        axis=0,
    )


def advance(state, base_plane, radial_full, table_azimuth, table_axial, damping_factor):
    local_z, azimuths, channels = state.shape
    radial_size = radial_full.shape[1]
    physical_m = jnp.einsum(
        "zmr,pm->pzr", state, table_azimuth, preferred_element_type=jnp.float32
    ).astype(jnp.bfloat16)
    arrived = lax.all_to_all(physical_m, "pencil", split_axis=0, concat_axis=1, tiled=True)
    physical = jnp.einsum("pzr,xz->pxr", arrived, table_axial, preferred_element_type=jnp.float32)
    product = (physical * base_plane.astype(jnp.float32)[..., None]).astype(jnp.bfloat16)
    returned = jnp.einsum(
        "pxr,xz->pzr", product, table_axial, preferred_element_type=jnp.float32
    ).astype(jnp.bfloat16)
    arrived_back = lax.all_to_all(returned, "pencil", split_axis=1, concat_axis=0, tiled=True)
    tendency = jnp.einsum(
        "pzr,pm->zmr", arrived_back, table_azimuth, preferred_element_type=jnp.float32
    )
    updated = (state.astype(jnp.float32) + step_size * tendency).astype(jnp.bfloat16)
    shaped = updated.reshape(local_z, azimuths, channels // radial_size, radial_size)
    applied = jnp.einsum(
        "zmkr,mor->zmko", shaped, radial_full, preferred_element_type=jnp.float32
    )
    return (applied * damping_factor[:, :, None, None]).reshape(state.shape).astype(jnp.bfloat16)


BLOCK = 16
VMEM_BYTES = 48 * 1024 * 1024


def swap_block(source, first, second):
    block = source[pl.ds(first, BLOCK), pl.ds(second, BLOCK), :].astype(jnp.float32)
    return jnp.swapaxes(block, 0, 1).astype(jnp.bfloat16)


def swap_all(source, target, rows, columns):
    def one(index, _):
        first = pl.multiple_of(index * BLOCK, BLOCK)
        for second in range(0, columns, BLOCK):
            target[pl.ds(second, BLOCK), pl.ds(first, BLOCK), :] = swap_block(source, first, second)
        return 0

    lax.fori_loop(0, rows // BLOCK, one, 0)


def analyse(state, table, spread, out, local_z, azimuths):
    def one(index, _):
        first = index * 4
        right = jnp.concatenate([state[first + j] for j in range(4)], axis=1)
        result = jnp.dot(table[...], right, preferred_element_type=jnp.float32)
        result = result.astype(jnp.bfloat16)
        for j in range(4):
            spread[first + j] = result[:, j * 128 : (j + 1) * 128]
        return 0

    lax.fori_loop(0, local_z // 4, one, 0)
    swap_all(spread, out, local_z, azimuths)


def start_kernel(state, table, out, spread):
    local_z, azimuths, _ = state.shape
    analyse(state, table, spread, out, local_z, azimuths)


def start_call(state, table_azimuth):
    local_z, azimuths, channels = state.shape
    vmem = pl.BlockSpec(memory_space=pltpu.VMEM)
    return pl.pallas_call(
        start_kernel,
        out_shape=jax.ShapeDtypeStruct((azimuths, local_z, channels), jnp.bfloat16),
        in_specs=[vmem, vmem],
        out_specs=vmem,
        scratch_shapes=[pltpu.VMEM(state.shape, jnp.bfloat16)],
        compiler_params=pltpu.CompilerParams(vmem_limit_bytes=VMEM_BYTES),
        cost_estimate=pl.CostEstimate(
            flops=2 * azimuths * state.size, bytes_accessed=6 * state.size, transcendentals=0
        ),
    )(state, table_azimuth)


def middle_kernel(arrived, base, table, table_t, out):
    pencils, count, local_z, channels = arrived.shape
    total_z = pencils * local_z
    right = jnp.concatenate(
        [arrived[:, j].reshape(total_z, channels) for j in range(count)], axis=1
    )
    physical = jnp.dot(table[...], right, preferred_element_type=jnp.float32)
    planes = jnp.concatenate(
        [jnp.broadcast_to(base[j], (channels, total_z)).T for j in range(count)], axis=1
    )
    product = (physical * planes).astype(jnp.bfloat16)
    back = jnp.dot(table_t[...], product, preferred_element_type=jnp.float32)
    back = back.astype(jnp.bfloat16)
    for j in range(count):
        out[:, j] = back[:, j * channels : (j + 1) * channels].reshape(pencils, local_z, channels)


def middle_call(arrived, base, table, table_t):
    pencils, points, local_z, channels = arrived.shape
    total_z = pencils * local_z
    count = 4
    block = pl.BlockSpec((pencils, count, local_z, channels), lambda p: (0, p, 0, 0))
    whole = pl.BlockSpec((total_z, total_z), lambda p: (0, 0))
    return pl.pallas_call(
        middle_kernel,
        grid=(points // count,),
        out_shape=jax.ShapeDtypeStruct(arrived.shape, jnp.bfloat16),
        in_specs=[block, pl.BlockSpec((count, 1, total_z), lambda p: (p, 0, 0)), whole, whole],
        out_specs=block,
        compiler_params=pltpu.CompilerParams(vmem_limit_bytes=VMEM_BYTES),
        cost_estimate=pl.CostEstimate(
            flops=4 * total_z * arrived.size, bytes_accessed=4 * arrived.size, transcendentals=0
        ),
    )(arrived, base, table, table_t)


def finish_kernel(
    last, active, back, state, radial, waves_squared, table, table_t, new_state, *rest
):
    out = None if last else rest[0]
    spread, by_mode = rest[-2:]
    local_z, azimuths, channels = state.shape
    half = azimuths // 2
    swap_all(back, spread, azimuths, local_z)

    def tendency(index, _):
        first = index * 4
        right = jnp.concatenate([spread[first + j] for j in range(4)], axis=1)
        result = jnp.dot(table_t[...], right, preferred_element_type=jnp.float32)
        for j in range(4):
            updated = state[first + j].astype(jnp.float32) + step_size * result[
                :, j * channels : (j + 1) * channels
            ]
            spread[first + j] = updated.astype(jnp.bfloat16)
        return 0

    lax.fori_loop(0, local_z // 4, tendency, 0)
    swap_all(spread, by_mode, local_z, azimuths)

    def radial_step(wave, first, count):
        left = by_mode[pl.ds(first, count)].reshape(count * local_z, channels)
        applied = jnp.dot(left, radial[wave], preferred_element_type=jnp.float32)
        wave_f = jnp.asarray(wave, jnp.int32).astype(jnp.float32)
        factor = 1.0 / (1.0 + viscosity * (waves_squared[...] + wave_f * wave_f))
        result = applied.reshape(count, local_z, channels) * factor[None]
        by_mode[pl.ds(first, count)] = result.astype(jnp.bfloat16)

    radial_step(0, 0, 1)
    radial_step(half, azimuths - 1, 1)
    group = 8
    loops = (half - 1) // group

    def several(index, _):
        for j in range(group):
            wave = 1 + index * group + j
            radial_step(wave, 2 * wave - 1, 2)
        return 0

    lax.fori_loop(0, loops, several, 0)
    for wave in range(1 + loops * group, half):
        radial_step(wave, 2 * wave - 1, 2)
    swap_all(by_mode, spread, azimuths, local_z)
    keep = active[0] > 0

    def choose(index, _):
        new_state[index] = jnp.where(keep, spread[index], state[index])
        return 0

    lax.fori_loop(0, local_z, choose, 0)
    if not last:
        analyse(new_state, table, spread, out, local_z, azimuths)


def finish_call(last, active, back, state, radial, waves_squared, table, table_t):
    local_z, azimuths, channels = state.shape
    vmem = pl.BlockSpec(memory_space=pltpu.VMEM)
    state_shape = jax.ShapeDtypeStruct(state.shape, jnp.bfloat16)
    out_shape = jax.ShapeDtypeStruct(back.shape, jnp.bfloat16)
    shapes = [state_shape] if last else [state_shape, out_shape]
    return pl.pallas_call(
        functools.partial(finish_kernel, last),
        out_shape=shapes,
        in_specs=[pl.BlockSpec(memory_space=pltpu.SMEM)] + [vmem] * 6,
        out_specs=[vmem] * len(shapes),
        scratch_shapes=[
            pltpu.VMEM(state.shape, jnp.bfloat16),
            pltpu.VMEM(back.shape, jnp.bfloat16),
        ],
        compiler_params=pltpu.CompilerParams(vmem_limit_bytes=VMEM_BYTES),
        cost_estimate=pl.CostEstimate(
            flops=4 * azimuths * state.size * 4, bytes_accessed=8 * state.size, transcendentals=0
        ),
    )(active, back, state, radial, waves_squared, table, table_t)


def run_kernels(states, base_wave, radial_inverse, step_counts, waves_axial, tables):
    segments = len(states)
    local_z, azimuths, channels = states[0].shape
    points = base_wave.shape[1]
    pencils = azimuths // points
    table_azimuth, table_axial = tables
    transposed = jnp.swapaxes(radial_inverse, 1, 2)
    blank = jnp.zeros_like(transposed)
    radial = transposed
    if channels != radial.shape[1]:
        radial = jnp.concatenate(
            [
                jnp.concatenate([transposed, blank], axis=2),
                jnp.concatenate([blank, transposed], axis=2),
            ],
            axis=1,
        )
    waves_f = waves_axial.astype(jnp.float32)
    waves_squared = jnp.broadcast_to((waves_f * waves_f)[:, None], (local_z, channels))
    base = base_wave.astype(jnp.float32)[:, :, None, :]
    shape = (pencils, points, local_z, channels)
    sent = [start_call(states[s], table_azimuth) for s in range(segments)]
    for step_index in range(NSTEP):
        last = step_index == NSTEP - 1
        for s in range(segments):
            arrived = lax.all_to_all(
                sent[s].reshape(shape), "pencil", split_axis=0, concat_axis=0, tiled=True
            )
            product = middle_call(arrived, base[s], table_axial, table_axial.T)
            back = lax.all_to_all(product, "pencil", split_axis=0, concat_axis=0, tiled=True)
            active = (step_index < step_counts[s : s + 1]).astype(jnp.int32)
            results = finish_call(
                last,
                active,
                back.reshape(azimuths, local_z, channels),
                states[s],
                radial,
                waves_squared,
                table_azimuth,
                table_azimuth.T,
            )
            states[s] = results[0]
            if not last:
                sent[s] = results[1]
    return states


def body(krylov_vector, base_wave, radial_inverse, step_counts, azimuth_shift, phase_tangent):
    segments, local_z, azimuths, channels = krylov_vector.shape
    total_z = local_z * lax.axis_size("pencil")
    table_azimuth = fourier_table(azimuths).astype(jnp.bfloat16)
    table_axial = fourier_table(total_z).astype(jnp.bfloat16)
    axial_index = lax.axis_index("pencil") * local_z + jnp.arange(local_z, dtype=jnp.int32)
    damping_factor = damping(axial_index, azimuths)
    radial_full = expand_radial(radial_inverse, azimuths)
    states = [krylov_vector[s] for s in range(segments)]
    fits = (
        local_z % BLOCK == 0
        and azimuths % BLOCK == 0
        and base_wave.shape[1] % 4 == 0
        and channels == 128
        and channels == 2 * radial_inverse.shape[1]
    )
    if fits:
        states = run_kernels(
            states,
            base_wave,
            radial_inverse,
            step_counts,
            (axial_index + 1) // 2,
            (table_azimuth, table_axial),
        )
    else:
        for step_index in range(NSTEP):
            for s in range(segments):
                advanced = advance(
                    states[s], base_wave[s], radial_full, table_azimuth, table_axial, damping_factor
                )
                states[s] = (
                    advanced
                    if step_index == 0
                    else jnp.where(step_index < step_counts[s], advanced, states[s])
                )
    table_full = fourier_table(azimuths)
    physical_last = jnp.einsum(
        "zmr,pm->zpr",
        states[-1].astype(jnp.float32),
        table_full,
        precision=lax.Precision.HIGHEST,
    )
    rolled = jnp.roll(physical_last, azimuth_shift[0], axis=1)
    shifted = jnp.einsum("zpr,pm->zmr", rolled, table_full, precision=lax.Precision.HIGHEST)
    shooting = jnp.stack(
        [
            states[s].astype(jnp.float32) - krylov_vector[s + 1].astype(jnp.float32)
            for s in range(segments - 1)
        ]
        + [shifted - krylov_vector[0].astype(jnp.float32)],
        axis=0,
    )
    local_phase = jnp.sum(phase_tangent.astype(jnp.float32) * krylov_vector[0].astype(jnp.float32))
    phase_value = lax.psum(local_phase, "pencil").reshape(1)
    return (shooting, phase_value)


def solution(mesh):
    return jax.shard_map(
        body,
        mesh=mesh,
        in_specs=(
            P("groups", "pencil", None, None),
            P("groups", "pencil", None),
            P("groups", None, None),
            P("groups"),
            P("groups"),
            P(("groups", "pencil"), None, None),
        ),
        out_specs=(P("groups", "pencil", None, None), P("groups")),
        check_vma=False,
    )
```

```python
import functools
import jax
import jax.numpy as jnp
from jax import lax
from jax.experimental import pallas as pl
from jax.experimental.pallas import tpu as pltpu
from jax.sharding import PartitionSpec as P

NSTEP = 3


viscosity = 2e-06
step_size = 0.4


def fourier_table(length):
    points = jnp.arange(length, dtype=jnp.int32)
    columns = jnp.arange(length, dtype=jnp.int32)
    wave_numbers = (columns + 1) // 2
    phase_index = points[:, None] * wave_numbers[None, :] % length
    angles = phase_index.astype(jnp.float32) * (2.0 * jnp.pi / length)
    cosine_col = (columns % 2 == 1) | (columns == 0)
    edge_col = (columns == 0) | (columns == length - 1)
    scales = jnp.where(
        edge_col, 1.0 / jnp.sqrt(jnp.float32(length)), jnp.sqrt(jnp.float32(2.0 / length))
    )
    values = jnp.where(cosine_col[None, :], jnp.cos(angles), jnp.sin(angles))
    return values * scales[None, :]


def damping(axial_index, azimuth_count):
    waves_axial = (axial_index + 1) // 2
    waves_azimuth = (jnp.arange(azimuth_count, dtype=jnp.int32) + 1) // 2
    squared_sum = (
        waves_axial[:, None] * waves_axial[:, None]
        + waves_azimuth[None, :] * waves_azimuth[None, :]
    )
    return 1.0 / (1.0 + viscosity * squared_sum.astype(jnp.float32))


def expand_radial(radial_table, azimuth_count):
    half_count = azimuth_count // 2
    return jnp.concatenate(
        [
            radial_table[:1],
            jnp.repeat(radial_table[1:half_count], 2, axis=0),
            radial_table[half_count : half_count + 1],
        ],
        axis=0,
    )


def advance(state, base_plane, radial_full, table_azimuth, table_axial, damping_factor):
    local_z, azimuths, channels = state.shape
    radial_size = radial_full.shape[1]
    physical_m = jnp.einsum(
        "zmr,pm->pzr", state, table_azimuth, preferred_element_type=jnp.float32
    ).astype(jnp.bfloat16)
    arrived = lax.all_to_all(physical_m, "pencil", split_axis=0, concat_axis=1, tiled=True)
    physical = jnp.einsum("pzr,xz->pxr", arrived, table_axial, preferred_element_type=jnp.float32)
    product = (physical * base_plane.astype(jnp.float32)[..., None]).astype(jnp.bfloat16)
    returned = jnp.einsum(
        "pxr,xz->pzr", product, table_axial, preferred_element_type=jnp.float32
    ).astype(jnp.bfloat16)
    arrived_back = lax.all_to_all(returned, "pencil", split_axis=1, concat_axis=0, tiled=True)
    tendency = jnp.einsum(
        "pzr,pm->zmr", arrived_back, table_azimuth, preferred_element_type=jnp.float32
    )
    updated = (state.astype(jnp.float32) + step_size * tendency).astype(jnp.bfloat16)
    shaped = updated.reshape(local_z, azimuths, channels // radial_size, radial_size)
    applied = jnp.einsum(
        "zmkr,mor->zmko", shaped, radial_full, preferred_element_type=jnp.float32
    )
    return (applied * damping_factor[:, :, None, None]).reshape(state.shape).astype(jnp.bfloat16)


BLOCK = 16
VMEM_BYTES = 48 * 1024 * 1024


def swap_block(source, first, second):
    if len(source.shape) == 4:
        block = source[first // BLOCK, :, pl.ds(second, BLOCK), :]
    else:
        block = source[pl.ds(first, BLOCK), pl.ds(second, BLOCK), :]
    block = block.astype(jnp.float32)
    return jnp.swapaxes(block, 0, 1).astype(jnp.bfloat16)


def swap_all(source, target, rows, columns):
    def one(index, _):
        first = pl.multiple_of(index * BLOCK, BLOCK)
        for second in range(0, columns, BLOCK):
            block = swap_block(source, first, second)
            if len(target.shape) == 4:
                target[second // BLOCK, :, pl.ds(first, BLOCK), :] = block
            else:
                target[pl.ds(second, BLOCK), pl.ds(first, BLOCK), :] = block
        return 0

    lax.fori_loop(0, rows // BLOCK, one, 0)


def analyse(state, table, spread, out, local_z, azimuths):
    def one(index, _):
        first = index * 4
        right = jnp.concatenate([state[first + j] for j in range(4)], axis=1)
        result = jnp.dot(table[...], right, preferred_element_type=jnp.float32)
        result = result.astype(jnp.bfloat16)
        for j in range(4):
            spread[first + j] = result[:, j * 128 : (j + 1) * 128]
        return 0

    lax.fori_loop(0, local_z // 4, one, 0)
    swap_all(spread, out, local_z, azimuths)


def start_kernel(state, table, out, spread):
    local_z, azimuths, _ = state.shape
    analyse(state, table, spread, out, local_z, azimuths)


def field_block(fields, offset):
    shape = (None,) + fields.shape[1:]
    return pl.BlockSpec(shape, lambda s: (s + offset, 0, 0, 0))


def sent_block(shape):
    pencils, _, points, local_z, channels = shape
    return pl.BlockSpec((pencils, None, points, local_z, channels), lambda s: (0, s, 0, 0, 0))


def whole_block(array):
    return pl.BlockSpec(array.shape, lambda s: (0,) * array.ndim)


def start_call(states, offset, table_azimuth, shape):
    _, local_z, azimuths, channels = states.shape
    size = shape[1] * local_z * azimuths * channels
    return pl.pallas_call(
        start_kernel,
        grid=(shape[1],),
        out_shape=jax.ShapeDtypeStruct(shape, jnp.bfloat16),
        in_specs=[field_block(states, offset), whole_block(table_azimuth)],
        out_specs=sent_block(shape),
        scratch_shapes=[pltpu.VMEM((local_z, azimuths, channels), jnp.bfloat16)],
        compiler_params=pltpu.CompilerParams(vmem_limit_bytes=VMEM_BYTES),
        cost_estimate=pl.CostEstimate(
            flops=2 * azimuths * size, bytes_accessed=6 * size, transcendentals=0
        ),
    )(states, table_azimuth)


def middle_kernel(arrived, base, table, table_t, out):
    pencils, count, local_z, channels = arrived.shape
    total_z = pencils * local_z
    right = jnp.concatenate(
        [arrived[:, j].reshape(total_z, channels) for j in range(count)], axis=1
    )
    physical = jnp.dot(table[...], right, preferred_element_type=jnp.float32)
    planes = jnp.concatenate(
        [jnp.broadcast_to(base[j], (channels, total_z)).T for j in range(count)], axis=1
    )
    product = (physical * planes).astype(jnp.bfloat16)
    back = jnp.dot(table_t[...], product, preferred_element_type=jnp.float32)
    back = back.astype(jnp.bfloat16)
    for j in range(count):
        out[:, j] = back[:, j * channels : (j + 1) * channels].reshape(pencils, local_z, channels)


def middle_call(arrived, base, table, table_t):
    pencils, group, points, local_z, channels = arrived.shape
    total_z = pencils * local_z
    count = 4
    block = pl.BlockSpec(
        (pencils, None, count, local_z, channels), lambda s, p: (0, s, p, 0, 0)
    )
    whole = pl.BlockSpec((total_z, total_z), lambda s, p: (0, 0))
    base_block = pl.BlockSpec((None, count, 1, total_z), lambda s, p: (s, p, 0, 0))
    return pl.pallas_call(
        middle_kernel,
        grid=(group, points // count),
        out_shape=jax.ShapeDtypeStruct(arrived.shape, jnp.bfloat16),
        in_specs=[block, base_block, whole, whole],
        out_specs=block,
        compiler_params=pltpu.CompilerParams(vmem_limit_bytes=VMEM_BYTES),
        cost_estimate=pl.CostEstimate(
            flops=4 * total_z * arrived.size, bytes_accessed=4 * arrived.size, transcendentals=0
        ),
    )(arrived, base, table, table_t)


def finish_kernel(
    last, active, back, state, radial, waves_squared, table, table_t, new_state, *rest
):
    out = None if last else rest[0]
    spread, by_mode = rest[-2:]
    local_z, azimuths, channels = state.shape
    half = azimuths // 2
    swap_all(back, spread, azimuths, local_z)

    def tendency(index, _):
        first = index * 4
        right = jnp.concatenate([spread[first + j] for j in range(4)], axis=1)
        result = jnp.dot(table_t[...], right, preferred_element_type=jnp.float32)
        for j in range(4):
            updated = state[first + j].astype(jnp.float32) + step_size * result[
                :, j * channels : (j + 1) * channels
            ]
            spread[first + j] = updated.astype(jnp.bfloat16)
        return 0

    lax.fori_loop(0, local_z // 4, tendency, 0)
    swap_all(spread, by_mode, local_z, azimuths)

    def radial_step(wave, first, count):
        left = by_mode[pl.ds(first, count)].reshape(count * local_z, channels)
        applied = jnp.dot(left, radial[wave], preferred_element_type=jnp.float32)
        wave_f = jnp.asarray(wave, jnp.int32).astype(jnp.float32)
        factor = 1.0 / (1.0 + viscosity * (waves_squared[...] + wave_f * wave_f))
        result = applied.reshape(count, local_z, channels) * factor[None]
        by_mode[pl.ds(first, count)] = result.astype(jnp.bfloat16)

    radial_step(0, 0, 1)
    radial_step(half, azimuths - 1, 1)
    group = 8
    loops = (half - 1) // group

    def several(index, _):
        for j in range(group):
            wave = 1 + index * group + j
            radial_step(wave, 2 * wave - 1, 2)
        return 0

    lax.fori_loop(0, loops, several, 0)
    for wave in range(1 + loops * group, half):
        radial_step(wave, 2 * wave - 1, 2)
    swap_all(by_mode, spread, azimuths, local_z)
    keep = active[pl.program_id(0)] > 0

    def choose(index, _):
        new_state[index] = jnp.where(keep, spread[index], state[index])
        return 0

    lax.fori_loop(0, local_z, choose, 0)
    if not last:
        analyse(new_state, table, spread, out, local_z, azimuths)


def finish_call(last, active, back, states, offset, radial, waves_squared, table, table_t):
    _, local_z, azimuths, channels = states.shape
    group = back.shape[1]
    fields = jax.ShapeDtypeStruct((group, local_z, azimuths, channels), jnp.bfloat16)
    shapes = [fields] if last else [fields, jax.ShapeDtypeStruct(back.shape, jnp.bfloat16)]
    blocks = [field_block(fields, 0)] + ([] if last else [sent_block(back.shape)])
    return pl.pallas_call(
        functools.partial(finish_kernel, last),
        grid=(group,),
        out_shape=shapes,
        in_specs=[
            pl.BlockSpec(memory_space=pltpu.SMEM),
            sent_block(back.shape),
            field_block(states, offset),
            whole_block(radial),
            whole_block(waves_squared),
            whole_block(table),
            whole_block(table_t),
        ],
        out_specs=blocks,
        scratch_shapes=[
            pltpu.VMEM((local_z, azimuths, channels), jnp.bfloat16),
            pltpu.VMEM((azimuths, local_z, channels), jnp.bfloat16),
        ],
        compiler_params=pltpu.CompilerParams(vmem_limit_bytes=VMEM_BYTES),
        cost_estimate=pl.CostEstimate(
            flops=16 * azimuths * fields.size, bytes_accessed=8 * fields.size, transcendentals=0
        ),
    )(active, back, states, radial, waves_squared, table, table_t)


def run_kernels(
    krylov_vector, base_wave, radial_inverse, step_counts, waves_axial, tables, phase_value
):
    segments, local_z, azimuths, channels = krylov_vector.shape
    points = base_wave.shape[1]
    pencils = azimuths // points
    table_azimuth, table_axial = tables
    transposed = jnp.swapaxes(radial_inverse, 1, 2)
    blank = jnp.zeros_like(transposed)
    radial = jnp.concatenate(
        [
            jnp.concatenate([transposed, blank], axis=2),
            jnp.concatenate([blank, transposed], axis=2),
        ],
        axis=1,
    )
    waves_f = waves_axial.astype(jnp.float32)
    waves_squared = jnp.broadcast_to((waves_f * waves_f)[:, None], (local_z, channels))
    base = base_wave.astype(jnp.float32)[:, :, None, :]
    later_table, phase_value = lax.optimization_barrier((table_azimuth, phase_value))
    first_size = (segments + 1) // 2
    groups = [(0, first_size), (first_size, segments)]
    states = [krylov_vector] * len(groups)
    offsets = [begin for begin, _ in groups]
    sent = [
        start_call(
            krylov_vector,
            begin,
            later_table if begin == 0 else table_azimuth,
            (pencils, end - begin, points, local_z, channels),
        )
        for begin, end in groups
    ]
    for step_index in range(NSTEP):
        last = step_index == NSTEP - 1
        for g, (begin, end) in enumerate(groups):
            arrived = lax.all_to_all(sent[g], "pencil", split_axis=0, concat_axis=0, tiled=True)
            product = middle_call(arrived, base[begin:end], table_axial, table_axial.T)
            back = lax.all_to_all(product, "pencil", split_axis=0, concat_axis=0, tiled=True)
            active = (step_index < step_counts[begin:end]).astype(jnp.int32)
            results = finish_call(
                last,
                active,
                back,
                states[g],
                offsets[g],
                radial,
                waves_squared,
                table_azimuth,
                table_azimuth.T,
            )
            states[g], offsets[g] = results[0], 0
            if not last:
                sent[g] = results[1]
    ends = [states[g][i] for g, (begin, end) in enumerate(groups) for i in range(end - begin)]
    return ends, phase_value


def body(krylov_vector, base_wave, radial_inverse, step_counts, azimuth_shift, phase_tangent):
    segments, local_z, azimuths, channels = krylov_vector.shape
    total_z = local_z * lax.axis_size("pencil")
    table_azimuth = fourier_table(azimuths).astype(jnp.bfloat16)
    table_axial = fourier_table(total_z).astype(jnp.bfloat16)
    axial_index = lax.axis_index("pencil") * local_z + jnp.arange(local_z, dtype=jnp.int32)
    damping_factor = damping(axial_index, azimuths)
    radial_full = expand_radial(radial_inverse, azimuths)
    states = [krylov_vector[s] for s in range(segments)]
    local_phase = jnp.sum(phase_tangent.astype(jnp.float32) * krylov_vector[0].astype(jnp.float32))
    phase_value = lax.psum(local_phase, "pencil").reshape(1)
    fits = (
        local_z % BLOCK == 0
        and azimuths % BLOCK == 0
        and base_wave.shape[1] == BLOCK
        and segments > 1
        and channels == 128
        and channels == 2 * radial_inverse.shape[1]
    )
    if fits:
        states, phase_value = run_kernels(
            krylov_vector,
            base_wave,
            radial_inverse,
            step_counts,
            (axial_index + 1) // 2,
            (table_azimuth, table_axial),
            phase_value,
        )
    else:
        for step_index in range(NSTEP):
            for s in range(segments):
                advanced = advance(
                    states[s], base_wave[s], radial_full, table_azimuth, table_axial, damping_factor
                )
                states[s] = (
                    advanced
                    if step_index == 0
                    else jnp.where(step_index < step_counts[s], advanced, states[s])
                )
    table_full = fourier_table(azimuths)
    physical_last = jnp.einsum(
        "zmr,pm->zpr",
        states[-1].astype(jnp.float32),
        table_full,
        precision=lax.Precision.HIGHEST,
    )
    rolled = jnp.roll(physical_last, azimuth_shift[0], axis=1)
    shifted = jnp.einsum("zpr,pm->zmr", rolled, table_full, precision=lax.Precision.HIGHEST)
    shooting = jnp.stack(
        [
            states[s].astype(jnp.float32) - krylov_vector[s + 1].astype(jnp.float32)
            for s in range(segments - 1)
        ]
        + [shifted - krylov_vector[0].astype(jnp.float32)],
        axis=0,
    )
    return (shooting, phase_value)


def solution(mesh):
    return jax.shard_map(
        body,
        mesh=mesh,
        in_specs=(
            P("groups", "pencil", None, None),
            P("groups", "pencil", None),
            P("groups", None, None),
            P("groups"),
            P("groups"),
            P(("groups", "pencil"), None, None),
        ),
        out_specs=(P("groups", "pencil", None, None), P("groups")),
        check_vma=False,
    )
```
